32 devices in a mesh: fsdp: 8 (over y, x, core), tensor: 4 (over z).
Axes of the slice: x: 2, y: 2, z: 4, core: 2. Of those that a mesh axis runs over, the one named last changes fastest.
Arguments:
- inputs: bfloat16 [2, 4096, 768], P(None, ('fsdp', 'tensor')), may hold values from -6 to 6
- cotangent: bfloat16 [2, 4096, 768], P(None, ('fsdp', 'tensor')), may hold values from -6 to 6
- segment_ids: int32 [2, 4096], P(None, 'fsdp'), may hold values from 0 to 3, as said below
- qkv_weight: float32 [768, 3, 768], P('fsdp', None, 'tensor'), may hold values from -0.21875 to 0.21875
- qkv_first: float32 [768, 3, 768], P('fsdp', None, 'tensor')
- qkv_second: float32 [768, 3, 768], P('fsdp', None, 'tensor'), as said below
- out_weight: float32 [768, 768], P('tensor', 'fsdp'), may hold values from -1.75 to 1.75
- out_first: float32 [768, 768], P('tensor', 'fsdp')
- out_second: float32 [768, 768], P('tensor', 'fsdp'), as said below
- up_weight: float32 [768, 3072], P('fsdp', 'tensor'), may hold values from -0.21875 to 0.21875
- up_first: float32 [768, 3072], P('fsdp', 'tensor')
- up_second: float32 [768, 3072], P('fsdp', 'tensor'), as said below
- down_weight: float32 [3072, 768], P('tensor', 'fsdp'), may hold values from -0.109375 to 0.109375
- down_first: float32 [3072, 768], P('tensor', 'fsdp')
- down_second: float32 [3072, 768], P('tensor', 'fsdp'), as said below
- vectors: float32 [8, 768], replicated, as said below
- vectors_first: float32 [8, 768], replicated
- vectors_second: float32 [8, 768], replicated, as said below
- unit_bias: float32 [3072], replicated, may hold values from -4 to 4
- unit_bias_first: float32 [3072], replicated
- unit_bias_second: float32 [3072], replicated, as said below
Outputs:
- layer_output: bfloat16 [2, 4096, 768], P(None, ('fsdp', 'tensor'))
- input_grad: float32 [2, 4096, 768], P(None, ('fsdp', 'tensor'))
- qkv_updated: float32 [768, 3, 768], P('fsdp', None, 'tensor')
- qkv_first_new: float32 [768, 3, 768], P('fsdp', None, 'tensor')
- qkv_second_new: float32 [768, 3, 768], P('fsdp', None, 'tensor')
- out_updated: float32 [768, 768], P('tensor', 'fsdp')
- out_first_new: float32 [768, 768], P('tensor', 'fsdp')
- out_second_new: float32 [768, 768], P('tensor', 'fsdp')
- up_updated: float32 [768, 3072], P('fsdp', 'tensor')
- up_first_new: float32 [768, 3072], P('fsdp', 'tensor')
- up_second_new: float32 [768, 3072], P('fsdp', 'tensor')
- down_updated: float32 [3072, 768], P('tensor', 'fsdp')
- down_first_new: float32 [3072, 768], P('tensor', 'fsdp')
- down_second_new: float32 [3072, 768], P('tensor', 'fsdp')
- vectors_updated: float32 [8, 768], replicated
- vectors_first_new: float32 [8, 768], replicated
- vectors_second_new: float32 [8, 768], replicated
- unit_bias_updated: float32 [3072], replicated
- unit_bias_first_new: float32 [3072], replicated
- unit_bias_second_new: float32 [3072], replicated
The draws below stay inside these ranges and needn't reach their ends.
Inputs may be any that keep to these rules, and one draw needn't show every extreme that they name: `segment_ids`: within each sequence of 512 positions the ids never fall and number its packed documents from 0; for each index of fsdp one of its 2 sequences is a single document. `vectors`: rows 4 and 6 are norms' gains, the other rows biases. `qkv_second`: Positive. `out_second`: Positive. `up_second`: Positive. `down_second`: Positive. `vectors_second`: Positive. `unit_bias_second`: Positive.
All inputs are finite; a program needn't handle non-finite values.
Results may differ from the reference program's by a relative error of at most 0.014.
The reference program's roundings to bfloat16 on the way count: a program that leaves them out, or rounds other values in their place, can miss the bound.
Values may be sent and summed in bfloat16 or wider, within the bound.
A program may use at most 128 MiB of HBM per device.

```python
import math
import jax
import jax.numpy as jnp
from jax import lax

D = 768
H = 12
HD = 64
FF = 3072
SEQ = 512
MICRO = 2
STEP = 3
SEQS_DEV = 1
TOK_MB = 4096


def grad_size(factor):
    return factor * math.sqrt(MICRO * TOK_MB)


def first_draw(key, dims_shape, factor):
    return 0.11 * grad_size(factor) * jax.random.normal(key, dims_shape, jnp.float32)


def second_draw(key, dims_shape, factor):
    magnitude = grad_size(factor)
    spread = jax.random.uniform(key, dims_shape, jnp.float32, 0.0, math.log(4.0))
    return 0.001 * magnitude * magnitude * jnp.exp(spread)


def draw_segment_ids(key, part):
    key = jax.random.fold_in(key, 11)
    group_total = TOK_MB // (SEQS_DEV * SEQ)
    per_group = MICRO * SEQS_DEV
    cut_key, pick_key = jax.random.split(key)
    boundaries = jax.random.randint(cut_key, (group_total, per_group, 3), 1, SEQ)
    chosen = jax.random.randint(pick_key, (group_total, 1, 1), 0, per_group)
    members = jnp.arange(per_group)[None, :, None]
    boundaries = jnp.where(members == chosen, SEQ, boundaries)
    positions = jnp.arange(SEQ)[None, None, :, None]
    segment_rows = jnp.sum((boundaries[:, :, None, :] <= positions).astype(jnp.int32), axis=-1)
    segment_rows = segment_rows.reshape(group_total, MICRO, SEQS_DEV, SEQ).transpose(1, 0, 2, 3)
    return segment_rows.reshape(MICRO, TOK_MB).astype(jnp.int32)


def draw_vectors(key, part):
    key = jax.random.fold_in(key, 23)
    normal_key, gain_key = jax.random.split(key)
    shifts = 0.3 * jax.random.normal(normal_key, (8, D), jnp.float32)
    gains = jax.random.uniform(gain_key, (8, D), jnp.float32, 0.6, 1.4)
    row_index = jnp.arange(8)
    is_gain = (row_index == 4) | (row_index == 6)
    return jnp.where(is_gain[:, None], gains, shifts)


def draw_qkv_first(key, part):
    key = jax.random.fold_in(key, 31)
    return first_draw(key, (D, 3, D), 0.4)


def draw_qkv_second(key, part):
    key = jax.random.fold_in(key, 32)
    return second_draw(key, (D, 3, D), 0.4)


def draw_out_first(key, part):
    key = jax.random.fold_in(key, 41)
    return first_draw(key, (D, D), 1.6 / math.sqrt(SEQ))


def draw_out_second(key, part):
    key = jax.random.fold_in(key, 42)
    return second_draw(key, (D, D), 1.6 / math.sqrt(SEQ))


def draw_up_first(key, part):
    key = jax.random.fold_in(key, 51)
    return first_draw(key, (D, FF), 0.3)


def draw_up_second(key, part):
    key = jax.random.fold_in(key, 52)
    return second_draw(key, (D, FF), 0.3)


def draw_down_first(key, part):
    key = jax.random.fold_in(key, 61)
    return first_draw(key, (FF, D), 0.6)


def draw_down_second(key, part):
    key = jax.random.fold_in(key, 62)
    return second_draw(key, (FF, D), 0.6)


def draw_vectors_first(key, part):
    key = jax.random.fold_in(key, 71)
    return first_draw(key, (8, D), 0.7)


def draw_vectors_second(key, part):
    key = jax.random.fold_in(key, 72)
    return second_draw(key, (8, D), 0.7)


def draw_unit_bias_first(key, part):
    key = jax.random.fold_in(key, 81)
    return first_draw(key, (FF,), 0.3)


def draw_unit_bias_second(key, part):
    key = jax.random.fold_in(key, 82)
    return second_draw(key, (FF,), 0.3)


def block_scale(stream_key, dims, cuts, low, largest):
    level, own = 1.0, jax.random.fold_in(stream_key, 6)
    for dim, blocks in cuts:
        steps = jnp.exp(jax.random.uniform(jax.random.fold_in(own, dim), (blocks,), jnp.float32, low / len(cuts), largest / len(cuts)))
        level = level * jnp.repeat(steps, dims[dim] // blocks).reshape([-1 if axis == dim else 1 for axis in range(len(dims))])
    return level


def gaussian(rng, dims, deviation, limit, cuts=(), held_as=jnp.bfloat16):
    drawn = deviation * jax.random.normal(rng, dims, jnp.float32)
    if cuts:
        drawn = drawn * block_scale(rng, dims, cuts, -0.22, 0.18)
    return jnp.clip(drawn, -limit, limit).astype(held_as)


def setup_inputs(seed: int = 0) -> dict:
    splits = jax.random.split(jax.random.key(seed), 22)
    return {
        "inputs": gaussian(splits[0], (MICRO, TOK_MB, D), 1.0, 6.0, ((1, 32),)),
        "cotangent": gaussian(splits[1], (MICRO, TOK_MB, D), 1.0, 6.0, ((1, 32),)),
        "segment_ids": draw_segment_ids(jax.random.fold_in(splits[21], 71), 0),
        "qkv_weight": gaussian(splits[3], (D, 3, D), D ** -0.5, 0.21875, ((0, 8), (2, 4)), jnp.float32),
        "qkv_first": draw_qkv_first(jax.random.fold_in(splits[21], 71), 0),
        "qkv_second": draw_qkv_second(jax.random.fold_in(splits[21], 71), 0),
        "out_weight": gaussian(splits[6], (D, D), (D * 8 // SEQ) ** -0.5, 1.75, ((0, 4), (1, 8)), jnp.float32),
        "out_first": draw_out_first(jax.random.fold_in(splits[21], 71), 0),
        "out_second": draw_out_second(jax.random.fold_in(splits[21], 71), 0),
        "up_weight": gaussian(splits[9], (D, FF), D ** -0.5, 0.21875, ((0, 8), (1, 4)), jnp.float32),
        "up_first": draw_up_first(jax.random.fold_in(splits[21], 71), 0),
        "up_second": draw_up_second(jax.random.fold_in(splits[21], 71), 0),
        "down_weight": gaussian(splits[12], (FF, D), FF ** -0.5, 0.109375, ((0, 4), (1, 8)), jnp.float32),
        "down_first": draw_down_first(jax.random.fold_in(splits[21], 71), 0),
        "down_second": draw_down_second(jax.random.fold_in(splits[21], 71), 0),
        "vectors": draw_vectors(jax.random.fold_in(splits[21], 71), 0),
        "vectors_first": draw_vectors_first(jax.random.fold_in(splits[21], 71), 0),
        "vectors_second": draw_vectors_second(jax.random.fold_in(splits[21], 71), 0),
        "unit_bias": gaussian(splits[18], (FF,), 0.3, 4.0, (), jnp.float32),
        "unit_bias_first": draw_unit_bias_first(jax.random.fold_in(splits[21], 71), 0),
        "unit_bias_second": draw_unit_bias_second(jax.random.fold_in(splits[21], 71), 0),
    }


HIGH = lax.Precision.HIGHEST
EPSILON = 1e-05
NEGATIVE = -1000000000.0
LEARNING_RATES = (0.03, 0.2, 0.03, 0.015, 0.1, 0.1)
WEIGHT_DECAYS = (0.01, 0.01, 0.01, 0.01, 0.0, 0.0)

@jax.custom_vjp
def low(v):
    return lax.optimization_barrier(v.astype(jnp.bfloat16)).astype(jnp.float32)

@jax.custom_vjp
def low_back(v):
    return v

def low_keep(v):
    return (low(v), None)

def low_pass(kept, grad):
    return (grad,)

def back_keep(v):
    return (v, None)

def back_low(kept, grad):
    return (low(grad),)
low.defvjp(low_keep, low_pass)
low_back.defvjp(back_keep, back_low)

def layer_norm(rows, gain, offset):
    center = rows - lax.optimization_barrier(jnp.mean(rows, axis=-1, keepdims=True))
    spread = lax.optimization_barrier(jnp.mean(center * center, axis=-1, keepdims=True))
    return center * lax.rsqrt(spread + EPSILON) * gain + offset

def attend(item):
    queries, key_rows, value_rows, segment_row = item
    scores = jnp.einsum('qhd,khd->hqk', queries, key_rows, precision=HIGH) * HD ** (-0.5)
    scores = low_back(scores)
    same_doc = segment_row[:, None] == segment_row[None, :]
    scores = jnp.where(same_doc[None], scores, NEGATIVE)
    probs = low(jax.nn.softmax(scores, axis=-1))
    return jnp.einsum('hqk,khd->qhd', probs, value_rows, precision=HIGH)

def forward(params, rows, segments):
    qkv_w, out_w, up_w, down_w, vectors, unit_bias = params
    qkv_low = low(qkv_w)
    out_low = low(out_w)
    up_low = low(up_w)
    down_low = low(down_w)
    mixed = jnp.einsum('nsd,dce->nsce', rows, qkv_low, precision=HIGH)
    queries = low(low_back(mixed[:, :, 0] + vectors[0]))
    key_rows = low(low_back(mixed[:, :, 1]))
    value_rows = low(low_back(mixed[:, :, 2] + vectors[1]))
    number = rows.shape[0]
    four_shape = (number, SEQ, H, HD)
    context = lax.map(jax.checkpoint(attend), (queries.reshape(four_shape), key_rows.reshape(four_shape), value_rows.reshape(four_shape), segments))
    context = low(low_back(context.reshape(number, SEQ, D)))
    branch = low_back(jnp.einsum('nsd,de->nse', context, out_low, precision=HIGH))
    first_norm = layer_norm(rows + branch + vectors[2], vectors[4], vectors[5])
    hidden = low_back(jnp.einsum('nsd,df->nsf', low(first_norm), up_low, precision=HIGH) + unit_bias)
    active = low(jax.nn.gelu(hidden, approximate=False))
    second = low_back(jnp.einsum('nsf,fd->nsd', active, down_low, precision=HIGH))
    return layer_norm(first_norm + second + vectors[3], vectors[6], vectors[7])

def adam_update(master, moment_one, moment_two, gradient, step_rate, decay_rate):
    one_new = 0.9 * moment_one + 0.1 * gradient
    two_new = 0.999 * moment_two + 0.001 * gradient * gradient
    one_hat = one_new / (1.0 - 0.9 ** STEP)
    two_hat = two_new / (1.0 - 0.999 ** STEP)
    updated = master - step_rate * (one_hat / (jnp.sqrt(two_hat) + 1e-08) + decay_rate * master)
    return (updated, one_new, two_new)

def reference(inputs, cotangent, segment_ids, qkv_weight, qkv_first, qkv_second, out_weight, out_first, out_second, up_weight, up_first, up_second, down_weight, down_first, down_second, vectors, vectors_first, vectors_second, unit_bias, unit_bias_first, unit_bias_second):
    params = (qkv_weight, out_weight, up_weight, down_weight, vectors, unit_bias)
    total_seqs = MICRO * TOK_MB // SEQ
    group_size = math.gcd(total_seqs, 8)
    group_count = total_seqs // group_size
    rows = inputs.astype(jnp.float32).reshape(group_count, group_size, SEQ, D)
    back_rows = cotangent.astype(jnp.float32).reshape(group_count, group_size, SEQ, D)
    segments = segment_ids.reshape(group_count, group_size, SEQ).astype(jnp.int32)

    def one_group(carry, item):
        block, back_block, segment_block = item
        result, pullback = jax.vjp(lambda weights, block_rows: forward(weights, block_rows, segment_block), params, block)
        grads, block_grad = pullback(back_block)
        carry = jax.tree.map(jnp.add, carry, grads)
        return (carry, (result.astype(jnp.bfloat16), block_grad))
    zero_grads = jax.tree.map(jnp.zeros_like, params)
    grads, (outputs, input_grads) = lax.scan(one_group, zero_grads, (rows, back_rows, segments))
    firsts = (qkv_first, out_first, up_first, down_first, vectors_first, unit_bias_first)
    seconds = (qkv_second, out_second, up_second, down_second, vectors_second, unit_bias_second)
    news = [adam_update(params[place], firsts[place], seconds[place], grads[place], LEARNING_RATES[place], WEIGHT_DECAYS[place]) for place in range(6)]
    layer_output = outputs.reshape(MICRO, TOK_MB, D)
    input_grad = input_grads.reshape(MICRO, TOK_MB, D)
    return (layer_output, input_grad, news[0][0], news[0][1], news[0][2], news[1][0], news[1][1], news[1][2], news[2][0], news[2][1], news[2][2], news[3][0], news[3][1], news[3][2], news[4][0], news[4][1], news[4][2], news[5][0], news[5][1], news[5][2])
```

```python
import jax
import jax.numpy as jnp
from jax import lax
from jax.experimental import pallas as pl
from jax.experimental.pallas import tpu as pltpu
from jax.sharding import PartitionSpec as P

HD = 64
SEQ = 512
MICRO = 2
STEP = 3


EPSILON = 1e-05
NEGATIVE = -1000000000.0
LEARNING_RATES = (0.03, 0.2, 0.03, 0.015, 0.1, 0.1)
WEIGHT_DECAYS = (0.01, 0.01, 0.01, 0.01, 0.0, 0.0)


def contract(left, right, left_dim, right_dim):
    return lax.dot_general(
        left, right, (((left_dim,), (right_dim,)), ((), ())), preferred_element_type=jnp.float32
    )


def gather_rows(shard):
    return lax.all_gather(shard, "tensor", axis=0, tiled=True)


def reduce_rows(left, right, right_dim):
    return lax.psum_scatter(
        contract(left, right, 1, right_dim), "tensor", scatter_dimension=0, tiled=True
    )


def norm_forward(rows, gain, offset):
    center = rows - jnp.mean(rows, axis=1, keepdims=True)
    inverse = lax.rsqrt(jnp.mean(center * center, axis=1, keepdims=True) + EPSILON)
    normed = center * inverse
    return (normed * gain + offset, normed, inverse)


def norm_backward(grad_out, normed, inverse, gain):
    scaled = grad_out * gain
    grad_rows = inverse * (
        scaled
        - jnp.mean(scaled, axis=1, keepdims=True)
        - normed * jnp.mean(scaled * normed, axis=1, keepdims=True)
    )
    return (grad_rows, jnp.sum(grad_out * normed, axis=0), jnp.sum(grad_out, axis=0))


BF = jnp.bfloat16
F32 = jnp.float32


def attend_forward_kernel(rows_ref, weight_ref, bias_ref, down_ref, across_ref, qkv_ref, context_ref):
    width = context_ref.shape[2]
    mixed = jnp.dot(rows_ref[0], weight_ref[...], preferred_element_type=F32) + bias_ref[...]
    low = mixed.astype(BF)
    qkv_ref[0] = low
    same_doc = down_ref[0] == across_ref[0]
    for start in range(0, width, HD):
        queries = low[:, start : start + HD]
        key_rows = low[:, width + start : width + start + HD]
        value_rows = low[:, 2 * width + start : 2 * width + start + HD]
        scores = contract(queries, key_rows, 1, 1) * HD ** (-0.5)
        scores = jnp.where(same_doc, scores, NEGATIVE)
        expos = jnp.exp(scores - jnp.max(scores, axis=1, keepdims=True))
        probs = expos / jnp.sum(expos, axis=1, keepdims=True)
        context = jnp.dot(probs.astype(BF), value_rows, preferred_element_type=F32)
        context_ref[0, :, start : start + HD] = context.astype(BF)


def attend_backward_kernel(
    rows_ref, weight_ref, qkv_ref, grad_ref, down_ref, across_ref, part_ref, weight_grad_ref, bias_grad_ref, mixed_ref
):
    width = grad_ref.shape[2]
    same_doc = down_ref[0] == across_ref[0]
    scale_factor = HD ** (-0.5)
    for start in range(0, width, HD):
        queries = qkv_ref[0, :, start : start + HD]
        key_rows = qkv_ref[0, :, width + start : width + start + HD]
        value_rows = qkv_ref[0, :, 2 * width + start : 2 * width + start + HD]
        grad_context = grad_ref[0, :, start : start + HD]
        scores = contract(key_rows, queries, 1, 1) * scale_factor
        scores = jnp.where(same_doc, scores, NEGATIVE)
        expos = jnp.exp(scores - jnp.max(scores, axis=0, keepdims=True))
        probs = expos / jnp.sum(expos, axis=0, keepdims=True)
        grad_probs = contract(value_rows, grad_context, 1, 1)
        inner = jnp.sum(probs * grad_probs, axis=0, keepdims=True)
        grad_scores = (probs * (grad_probs - inner)).astype(BF)
        mixed_ref[:, start : start + HD] = (contract(grad_scores, key_rows, 0, 0) * scale_factor).astype(BF)
        mixed_ref[:, width + start : width + start + HD] = (
            jnp.dot(grad_scores, queries, preferred_element_type=F32) * scale_factor
        ).astype(BF)
        mixed_ref[:, 2 * width + start : 2 * width + start + HD] = jnp.dot(
            probs.astype(BF), grad_context, preferred_element_type=F32
        ).astype(BF)
    mixed = mixed_ref[...]
    part_ref[0] = contract(mixed, weight_ref[...], 1, 1).astype(part_ref.dtype)
    weight_part = contract(rows_ref[0], mixed, 0, 0)
    bias_part = jnp.sum(mixed.astype(F32), axis=0, keepdims=True)

    @pl.when(pl.program_id(0) == 0)
    def _():
        weight_grad_ref[...] = weight_part
        bias_grad_ref[...] = bias_part

    @pl.when(pl.program_id(0) > 0)
    def _():
        weight_grad_ref[...] += weight_part
        bias_grad_ref[...] += bias_part


def by_sequence(shape):
    return pl.BlockSpec((1,) + shape, lambda item: (item, 0, 0))


def shared_block(shape):
    return pl.BlockSpec(shape, lambda item: (0, 0))


def attend_forward(rows, weight, bias, down_ids, across_ids):
    count, length, model = rows.shape
    triple = weight.shape[1]
    width = triple // 3
    return pl.pallas_call(
        attend_forward_kernel,
        grid=(count,),
        in_specs=[
            by_sequence((length, model)),
            shared_block((model, triple)),
            shared_block((1, triple)),
            by_sequence((length, 1)),
            by_sequence((1, length)),
        ],
        out_specs=[by_sequence((length, triple)), by_sequence((length, width))],
        out_shape=[
            jax.ShapeDtypeStruct((count, length, triple), BF),
            jax.ShapeDtypeStruct((count, length, width), BF),
        ],
        compiler_params=pltpu.CompilerParams(vmem_limit_bytes=48 * 2**20),
        name="attend_forward",
    )(rows, weight, bias, down_ids, across_ids)


def attend_backward(rows, weight, qkv, grad_context, down_ids, across_ids):
    count, length, model = rows.shape
    triple = weight.shape[1]
    width = triple // 3
    return pl.pallas_call(
        attend_backward_kernel,
        grid=(count,),
        in_specs=[
            by_sequence((length, model)),
            shared_block((model, triple)),
            by_sequence((length, triple)),
            by_sequence((length, width)),
            by_sequence((length, 1)),
            by_sequence((1, length)),
        ],
        out_specs=[by_sequence((length, model)), shared_block((model, triple)), shared_block((1, triple))],
        out_shape=[
            jax.ShapeDtypeStruct((count, length, model), BF),
            jax.ShapeDtypeStruct((model, triple), F32),
            jax.ShapeDtypeStruct((1, triple), F32),
        ],
        scratch_shapes=[pltpu.VMEM((length, triple), BF)],
        compiler_params=pltpu.CompilerParams(vmem_limit_bytes=48 * 2**20),
        name="attend_backward",
    )(rows, weight, qkv, grad_context, down_ids, across_ids)


def adam_update(master, moment_one, moment_two, gradient, step_rate, decay_rate):
    one_new = 0.9 * moment_one + 0.1 * gradient
    two_new = 0.999 * moment_two + 0.001 * gradient * gradient
    one_hat = one_new / (1.0 - 0.9**STEP)
    two_hat = two_new / (1.0 - 0.999**STEP)
    updated = master - step_rate * (one_hat / (jnp.sqrt(two_hat) + 1e-08) + decay_rate * master)
    return (updated, one_new, two_new)


def shards(
    inputs,
    cotangent,
    segment_ids,
    qkv_weight,
    qkv_first,
    qkv_second,
    out_weight,
    out_first,
    out_second,
    up_weight,
    up_first,
    up_second,
    down_weight,
    down_first,
    down_second,
    vectors,
    vectors_first,
    vectors_second,
    unit_bias,
    unit_bias_first,
    unit_bias_second,
):
    tensor_rank = lax.axis_index("tensor")
    model = inputs.shape[2]
    head_width = qkv_weight.shape[2]
    unit_width = up_weight.shape[1]
    head_start = tensor_rank * head_width
    unit_start = tensor_rank * unit_width
    triple = 3 * head_width
    unit_slice = lax.dynamic_slice_in_dim(unit_bias, unit_start, unit_width, 0)
    head_slices = lax.dynamic_slice_in_dim(vectors[:2], head_start, head_width, 1)
    qkv_bias = jnp.concatenate([head_slices[0], jnp.zeros((head_width,), F32), head_slices[1]])[None]
    micro_count, local_count, _ = inputs.shape

    def gather(rows):
        return lax.all_gather(rows.astype(BF), "tensor", axis=1, tiled=True)

    def scatter(partial):
        return lax.psum_scatter(partial.astype(BF), "tensor", scatter_dimension=1, tiled=True).astype(F32)

    def flat(rows):
        return rows.reshape(-1, rows.shape[-1])

    def unflat(rows):
        return rows.reshape(micro_count, -1, rows.shape[-1])

    qkv_flat = lax.all_gather(
        qkv_weight.reshape(-1, triple).astype(BF), "fsdp", axis=0, tiled=True
    )
    others = lax.all_gather(
        jnp.concatenate([out_weight.T, up_weight, down_weight.T], axis=1).astype(BF), "fsdp", axis=0, tiled=True
    )
    out_turned = others[:, :head_width]
    up_full = others[:, head_width : head_width + unit_width]
    down_turned = others[:, head_width + unit_width :]

    whole = gather(inputs)
    length = whole.shape[1]
    sequences = whole.reshape(-1, SEQ, model)
    ids = segment_ids.reshape(-1, SEQ)
    down_ids, across_ids = ids[:, :, None], ids[:, None, :]
    qkv_rows, context = attend_forward(sequences, qkv_flat, qkv_bias, down_ids, across_ids)
    context_flat = flat(context)
    branch = scatter(unflat(contract(context_flat, out_turned, 1, 1)))
    residual_one = flat(inputs).astype(F32) + flat(branch) + vectors[2]
    first_norm, normed_one, inverse_one = norm_forward(residual_one, vectors[4], vectors[5])
    first_whole = flat(gather(unflat(first_norm.astype(BF))))
    hidden = jnp.dot(first_whole, up_full, preferred_element_type=F32) + unit_slice
    active_float, gelu_pull = jax.vjp(lambda pre_act: jax.nn.gelu(pre_act, approximate=False), hidden)
    active = active_float.astype(BF)
    second = flat(scatter(unflat(contract(active, down_turned, 1, 1))))
    residual_two = first_norm + second + vectors[3]
    result_rows, normed_two, inverse_two = norm_forward(residual_two, vectors[6], vectors[7])
    layer_output = unflat(result_rows.astype(BF))
    back_rows = flat(cotangent).astype(F32)
    grad_two, gain_two_grad, offset_two_grad = norm_backward(back_rows, normed_two, inverse_two, vectors[6])
    down_bias_grad = jnp.sum(grad_two, axis=0)
    grad_branch_two = flat(gather(unflat(grad_two.astype(BF))))
    grad_active = jnp.dot(grad_branch_two, down_turned, preferred_element_type=F32)
    grad_hidden = gelu_pull(grad_active)[0].astype(BF)
    first_back = scatter(unflat(contract(grad_hidden, up_full, 1, 1)))
    down_grad = contract(grad_branch_two, active, 0, 0)
    up_grad = contract(first_whole, grad_hidden, 0, 0)
    unit_part = jnp.sum(grad_hidden.astype(F32), axis=0)
    wide_total = lax.psum_scatter(
        jnp.concatenate([up_grad, down_grad], axis=1).astype(BF), "fsdp", scatter_dimension=0, tiled=True
    ).astype(F32)
    grad_first = grad_two + flat(first_back)
    grad_one, gain_one_grad, offset_one_grad = norm_backward(grad_first, normed_one, inverse_one, vectors[4])
    out_bias_grad = jnp.sum(grad_one, axis=0)
    grad_branch_one = flat(gather(unflat(grad_one.astype(BF))))
    grad_context = jnp.dot(grad_branch_one, out_turned, preferred_element_type=F32).astype(BF)
    out_grad = contract(grad_branch_one, context_flat, 0, 0)
    input_parts, qkv_grad, qkv_bias_grad = attend_backward(
        sequences, qkv_flat, qkv_rows, grad_context.reshape(context.shape), down_ids, across_ids
    )
    input_grad = unflat(grad_one + flat(scatter(input_parts.reshape(micro_count, length, model))))
    narrow_total = lax.psum_scatter(
        jnp.concatenate([qkv_grad, out_grad], axis=1).astype(BF), "fsdp", scatter_dimension=0, tiled=True
    ).astype(F32)
    zero_rows = jnp.zeros((2, model), F32)
    qv_grad = lax.dynamic_update_slice_in_dim(
        zero_rows, jnp.concatenate([qkv_bias_grad[:, :head_width], qkv_bias_grad[:, 2 * head_width :]], axis=0), head_start, 1
    )
    vector_grad = jnp.concatenate(
        [
            qv_grad,
            jnp.stack(
                [
                    out_bias_grad,
                    down_bias_grad,
                    gain_one_grad,
                    offset_one_grad,
                    gain_two_grad,
                    offset_two_grad,
                ],
                axis=0,
            ),
        ],
        axis=0,
    )
    unit_grad = lax.dynamic_update_slice_in_dim(jnp.zeros(unit_bias.shape, F32), unit_part, unit_start, 0)
    small = lax.psum(jnp.concatenate([vector_grad, unit_grad.reshape(-1, model)], axis=0), ("fsdp", "tensor"))
    grad_totals = (
        narrow_total[:, :triple].reshape(qkv_weight.shape),
        narrow_total[:, triple:].T,
        wide_total[:, :unit_width],
        wide_total[:, unit_width:].T,
    )
    vector_total, unit_total = small[:8], small[8:].reshape(unit_bias.shape)
    masters = (qkv_weight, out_weight, up_weight, down_weight, vectors, unit_bias)
    firsts = (qkv_first, out_first, up_first, down_first, vectors_first, unit_bias_first)
    seconds = (qkv_second, out_second, up_second, down_second, vectors_second, unit_bias_second)
    gradients = (
        grad_totals[0],
        grad_totals[1],
        grad_totals[2],
        grad_totals[3],
        vector_total,
        unit_total,
    )
    news = [
        adam_update(
            masters[place],
            firsts[place],
            seconds[place],
            gradients[place],
            LEARNING_RATES[place],
            WEIGHT_DECAYS[place],
        )
        for place in range(6)
    ]
    return (
        layer_output,
        input_grad,
        news[0][0],
        news[0][1],
        news[0][2],
        news[1][0],
        news[1][1],
        news[1][2],
        news[2][0],
        news[2][1],
        news[2][2],
        news[3][0],
        news[3][1],
        news[3][2],
        news[4][0],
        news[4][1],
        news[4][2],
        news[5][0],
        news[5][1],
        news[5][2],
    )


def solution(mesh):
    placed = (
        P(None, ("fsdp", "tensor"), None),
        P(None, ("fsdp", "tensor"), None),
        P(None, "fsdp"),
        P("fsdp", None, "tensor"),
        P("fsdp", None, "tensor"),
        P("fsdp", None, "tensor"),
        P("tensor", "fsdp"),
        P("tensor", "fsdp"),
        P("tensor", "fsdp"),
        P("fsdp", "tensor"),
        P("fsdp", "tensor"),
        P("fsdp", "tensor"),
        P("tensor", "fsdp"),
        P("tensor", "fsdp"),
        P("tensor", "fsdp"),
        P(),
        P(),
        P(),
        P(),
        P(),
        P(),
    )
    return jax.shard_map(
        shards,
        mesh=mesh,
        in_specs=placed,
        out_specs=(
            P(None, ("fsdp", "tensor"), None),
            P(None, ("fsdp", "tensor"), None),
            P("fsdp", None, "tensor"),
            P("fsdp", None, "tensor"),
            P("fsdp", None, "tensor"),
            P("tensor", "fsdp"),
            P("tensor", "fsdp"),
            P("tensor", "fsdp"),
            P("fsdp", "tensor"),
            P("fsdp", "tensor"),
            P("fsdp", "tensor"),
            P("tensor", "fsdp"),
            P("tensor", "fsdp"),
            P("tensor", "fsdp"),
            P(),
            P(),
            P(),
            P(),
            P(),
            P(),
        ),
        check_vma=False,
    )
```

```python
import jax
import jax.numpy as jnp
from jax import lax
from jax.experimental import pallas as pl
from jax.experimental.pallas import tpu as pltpu
from jax.sharding import Mesh
from jax.sharding import PartitionSpec as P

HD = 64
SEQ = 512
MICRO = 2
STEP = 3


EPSILON = 1e-05
NEGATIVE = -1000000000.0
LEARNING_RATES = (0.03, 0.2, 0.03, 0.015, 0.1, 0.1)
WEIGHT_DECAYS = (0.01, 0.01, 0.01, 0.01, 0.0, 0.0)


def contract(left, right, left_dim, right_dim):
    return lax.dot_general(
        left, right, (((left_dim,), (right_dim,)), ((), ())), preferred_element_type=jnp.float32
    )


def gather_rows(shard):
    return lax.all_gather(shard, "tensor", axis=0, tiled=True)


def reduce_rows(left, right, right_dim):
    return lax.psum_scatter(
        contract(left, right, 1, right_dim), "tensor", scatter_dimension=0, tiled=True
    )


def norm_forward(rows, gain, offset):
    center = rows - jnp.mean(rows, axis=1, keepdims=True)
    inverse = lax.rsqrt(jnp.mean(center * center, axis=1, keepdims=True) + EPSILON)
    normed = center * inverse
    return (normed * gain + offset, normed, inverse)


def norm_backward(grad_out, normed, inverse, gain):
    scaled = grad_out * gain
    grad_rows = inverse * (
        scaled
        - jnp.mean(scaled, axis=1, keepdims=True)
        - normed * jnp.mean(scaled * normed, axis=1, keepdims=True)
    )
    return (grad_rows, jnp.sum(grad_out * normed, axis=0), jnp.sum(grad_out, axis=0))


FSDP = ("chip", "core")
BF = jnp.bfloat16
F32 = jnp.float32


def attend_forward_kernel(rows_ref, weight_ref, bias_ref, down_ref, across_ref, qkv_ref, context_ref):
    width = context_ref.shape[2]
    mixed = jnp.dot(rows_ref[0], weight_ref[...], preferred_element_type=F32) + bias_ref[...]
    low = mixed.astype(BF)
    qkv_ref[0] = low
    same_doc = down_ref[0] == across_ref[0]
    for start in range(0, width, HD):
        queries = low[:, start : start + HD]
        key_rows = low[:, width + start : width + start + HD]
        value_rows = low[:, 2 * width + start : 2 * width + start + HD]
        scores = contract(queries, key_rows, 1, 1) * HD ** (-0.5)
        scores = jnp.where(same_doc, scores, NEGATIVE)
        expos = jnp.exp(scores - jnp.max(scores, axis=1, keepdims=True))
        probs = expos / jnp.sum(expos, axis=1, keepdims=True)
        context = jnp.dot(probs.astype(BF), value_rows, preferred_element_type=F32)
        context_ref[0, :, start : start + HD] = context.astype(BF)


def attend_backward_kernel(
    rows_ref, weight_ref, qkv_ref, grad_ref, down_ref, across_ref, part_ref, weight_grad_ref, bias_grad_ref, mixed_ref
):
    width = grad_ref.shape[2]
    same_doc = down_ref[0] == across_ref[0]
    scale_factor = HD ** (-0.5)
    for start in range(0, width, HD):
        queries = qkv_ref[0, :, start : start + HD]
        key_rows = qkv_ref[0, :, width + start : width + start + HD]
        value_rows = qkv_ref[0, :, 2 * width + start : 2 * width + start + HD]
        grad_context = grad_ref[0, :, start : start + HD]
        scores = contract(key_rows, queries, 1, 1) * scale_factor
        scores = jnp.where(same_doc, scores, NEGATIVE)
        expos = jnp.exp(scores - jnp.max(scores, axis=0, keepdims=True))
        probs = expos / jnp.sum(expos, axis=0, keepdims=True)
        grad_probs = contract(value_rows, grad_context, 1, 1)
        inner = jnp.sum(probs * grad_probs, axis=0, keepdims=True)
        grad_scores = (probs * (grad_probs - inner)).astype(BF)
        mixed_ref[:, start : start + HD] = (contract(grad_scores, key_rows, 0, 0) * scale_factor).astype(BF)
        mixed_ref[:, width + start : width + start + HD] = (
            jnp.dot(grad_scores, queries, preferred_element_type=F32) * scale_factor
        ).astype(BF)
        mixed_ref[:, 2 * width + start : 2 * width + start + HD] = jnp.dot(
            probs.astype(BF), grad_context, preferred_element_type=F32
        ).astype(BF)
    mixed = mixed_ref[...]
    part_ref[0] = contract(mixed, weight_ref[...], 1, 1).astype(part_ref.dtype)
    weight_part = contract(rows_ref[0], mixed, 0, 0)
    bias_part = jnp.sum(mixed.astype(F32), axis=0, keepdims=True)

    @pl.when(pl.program_id(0) == 0)
    def _():
        weight_grad_ref[...] = weight_part
        bias_grad_ref[...] = bias_part

    @pl.when(pl.program_id(0) > 0)
    def _():
        weight_grad_ref[...] += weight_part
        bias_grad_ref[...] += bias_part


def by_sequence(shape):
    return pl.BlockSpec((1,) + shape, lambda item: (item, 0, 0))


def shared_block(shape):
    return pl.BlockSpec(shape, lambda item: (0, 0))


def attend_forward(rows, weight, bias, down_ids, across_ids):
    count, length, model = rows.shape
    triple = weight.shape[1]
    width = triple // 3
    return pl.pallas_call(
        attend_forward_kernel,
        grid=(count,),
        in_specs=[
            by_sequence((length, model)),
            shared_block((model, triple)),
            shared_block((1, triple)),
            by_sequence((length, 1)),
            by_sequence((1, length)),
        ],
        out_specs=[by_sequence((length, triple)), by_sequence((length, width))],
        out_shape=[
            jax.ShapeDtypeStruct((count, length, triple), BF),
            jax.ShapeDtypeStruct((count, length, width), BF),
        ],
        compiler_params=pltpu.CompilerParams(vmem_limit_bytes=48 * 2**20),
        name="attend_forward",
    )(rows, weight, bias, down_ids, across_ids)


def attend_backward(rows, weight, qkv, grad_context, down_ids, across_ids):
    count, length, model = rows.shape
    triple = weight.shape[1]
    width = triple // 3
    return pl.pallas_call(
        attend_backward_kernel,
        grid=(count,),
        in_specs=[
            by_sequence((length, model)),
            shared_block((model, triple)),
            by_sequence((length, triple)),
            by_sequence((length, width)),
            by_sequence((length, 1)),
            by_sequence((1, length)),
        ],
        out_specs=[by_sequence((length, model)), shared_block((model, triple)), shared_block((1, triple))],
        out_shape=[
            jax.ShapeDtypeStruct((count, length, model), BF),
            jax.ShapeDtypeStruct((model, triple), F32),
            jax.ShapeDtypeStruct((1, triple), F32),
        ],
        scratch_shapes=[pltpu.VMEM((length, triple), BF)],
        compiler_params=pltpu.CompilerParams(vmem_limit_bytes=48 * 2**20),
        name="attend_backward",
    )(rows, weight, qkv, grad_context, down_ids, across_ids)


def adam_update(master, moment_one, moment_two, gradient, step_rate, decay_rate):
    one_new = 0.9 * moment_one + 0.1 * gradient
    two_new = 0.999 * moment_two + 0.001 * gradient * gradient
    one_hat = one_new / (1.0 - 0.9**STEP)
    two_hat = two_new / (1.0 - 0.999**STEP)
    updated = master - step_rate * (one_hat / (jnp.sqrt(two_hat) + 1e-08) + decay_rate * master)
    return (updated, one_new, two_new)


def shards(
    inputs,
    cotangent,
    segment_ids,
    qkv_weight,
    qkv_first,
    qkv_second,
    out_weight,
    out_first,
    out_second,
    up_weight,
    up_first,
    up_second,
    down_weight,
    down_first,
    down_second,
    vectors,
    vectors_first,
    vectors_second,
    unit_bias,
    unit_bias_first,
    unit_bias_second,
):
    tensor_rank = lax.axis_index("tensor")
    model = inputs.shape[2]
    head_width = qkv_weight.shape[2]
    unit_width = up_weight.shape[1]
    head_start = tensor_rank * head_width
    triple = 3 * head_width
    chip_count = lax.axis_size("chip")
    tensor_count = lax.axis_size("tensor")
    core_rank = lax.axis_index("core")
    half_width = unit_width // 2
    depth = up_weight.shape[0]
    unit_slice = lax.dynamic_index_in_dim(
        unit_bias.reshape(tensor_count, 2, half_width), core_rank, 1, keepdims=False
    ).reshape(-1)
    head_slices = lax.dynamic_slice_in_dim(vectors[:2], head_start, head_width, 1)
    qkv_bias = jnp.concatenate([head_slices[0], jnp.zeros((head_width,), F32), head_slices[1]])[None]
    micro_count, local_count, _ = inputs.shape

    def shifted(rows, step):
        pairs = [(place, (place + step) % tensor_count) for place in range(tensor_count)]
        return lax.ppermute(rows, "tensor", pairs)

    def gather(rows):
        rows = rows.astype(BF)
        whole_rows = jnp.zeros((rows.shape[0], tensor_count) + rows.shape[1:], BF)
        for step in range(tensor_count):
            part = shifted(rows, step) if step else rows
            source = lax.rem(tensor_rank + tensor_count - step, tensor_count)
            whole_rows = lax.dynamic_update_slice_in_dim(whole_rows, part[:, None], source, 1)
        return whole_rows.reshape(rows.shape[0], -1, rows.shape[2])

    def scatter(partial):
        parts = partial.astype(BF).reshape(partial.shape[0], tensor_count, -1, partial.shape[2])
        total = lax.dynamic_index_in_dim(parts, tensor_rank, 1, keepdims=False).astype(F32)
        for step in range(1, tensor_count):
            target = lax.rem(tensor_rank + step, tensor_count)
            block = lax.dynamic_index_in_dim(parts, target, 1, keepdims=False)
            total = total + shifted(block, step).astype(F32)
        return total

    def swap(rows):
        return lax.ppermute(rows.astype(BF), "core", [(0, 1), (1, 0)])

    def both(rows):
        return jnp.concatenate([rows, swap(rows)], axis=0)

    def join(partial):
        count = partial.shape[0] // 2
        return partial[:count] + swap(partial[count:]).astype(F32)

    def by_core(mine, other, axis):
        first_part = jnp.where(core_rank == 0, mine, other)
        second_part = jnp.where(core_rank == 0, other, mine)
        return jnp.concatenate([first_part, second_part], axis=axis)

    def sum_everywhere(rows):
        for name in ("core", "chip", "tensor"):
            size = lax.axis_size(name)
            if size & (size - 1):
                rows = lax.psum(rows, name)
                continue
            step = 1
            while step < size:
                rows = rows + lax.ppermute(rows, name, [(place, place ^ step) for place in range(size)])
                step *= 2
        return rows

    def half(halves, rank, axis):
        return lax.dynamic_index_in_dim(halves, rank, axis, keepdims=False)

    def flat(rows):
        return rows.reshape(-1, rows.shape[-1])

    def unflat(rows):
        return rows.reshape(micro_count, -1, rows.shape[-1])

    whole = gather(inputs)
    narrow = lax.all_gather(
        jnp.concatenate([qkv_weight.reshape(-1, triple), out_weight.T], axis=1).astype(BF), FSDP, axis=0, tiled=True
    )
    qkv_flat = narrow[:, :triple]
    out_turned = narrow[:, triple:]
    wide_shard = jnp.stack([up_weight, down_weight.T], axis=1).astype(BF).reshape(depth, 2, 2, half_width)
    wide_mine = half(wide_shard, core_rank, 2)
    wide_other = swap(half(wide_shard, 1 - core_rank, 2))
    wide_block = by_core(wide_mine, wide_other, 0).reshape(2 * depth, 2 * half_width)
    wide_full = lax.all_gather(lax.all_gather(wide_block, "tensor"), "chip")
    up_full, down_turned = (
        jnp.concatenate(
            [
                wide_full[:, place, :, start : start + half_width].reshape(model, half_width)
                for place in range(tensor_count)
            ],
            axis=1,
        )
        for start in (0, half_width)
    )
    length = whole.shape[1]
    sequences = whole.reshape(-1, SEQ, model)
    ids = segment_ids.reshape(-1, SEQ)
    down_ids, across_ids = ids[:, :, None], ids[:, None, :]
    qkv_rows, context = attend_forward(sequences, qkv_flat, qkv_bias, down_ids, across_ids)
    context_flat = flat(context)
    branch = scatter(unflat(contract(context_flat, out_turned, 1, 1)))
    residual_one = flat(inputs).astype(F32) + flat(branch) + vectors[2]
    first_norm, normed_one, inverse_one = norm_forward(residual_one, vectors[4], vectors[5])
    first_whole = both(first_norm.astype(BF))
    hidden = jnp.dot(first_whole, up_full, preferred_element_type=F32) + unit_slice
    active_float, gelu_pull = jax.vjp(lambda pre_act: jax.nn.gelu(pre_act, approximate=False), hidden)
    active = active_float.astype(BF)
    second = join(contract(active, down_turned, 1, 1))
    residual_two = first_norm + second + vectors[3]
    result_rows, normed_two, inverse_two = norm_forward(residual_two, vectors[6], vectors[7])
    layer_output = unflat(result_rows.astype(BF))
    back_rows = flat(cotangent).astype(F32)
    grad_two, gain_two_grad, offset_two_grad = norm_backward(back_rows, normed_two, inverse_two, vectors[6])
    down_bias_grad = jnp.sum(grad_two, axis=0)
    grad_branch_two = both(grad_two.astype(BF))
    grad_active = jnp.dot(grad_branch_two, down_turned, preferred_element_type=F32)
    grad_hidden = gelu_pull(grad_active)[0].astype(BF)
    first_back = join(contract(grad_hidden, up_full, 1, 1))
    down_grad = contract(grad_branch_two, active, 0, 0)
    up_grad = contract(first_whole, grad_hidden, 0, 0)
    unit_part = jnp.sum(grad_hidden.astype(F32), axis=0)
    up_low, down_low = up_grad.astype(BF), down_grad.astype(BF)
    wide_grad = jnp.concatenate(
        [
            jnp.concatenate(
                [low[:, start : start + half_width] for low in (up_low, down_low)], axis=1
            ).reshape(chip_count, 2 * depth, 2 * half_width)
            for start in range(0, tensor_count * half_width, half_width)
        ],
        axis=1,
    )
    wide_part = lax.psum_scatter(wide_grad, "chip", scatter_dimension=0, tiled=False)
    wide_part = lax.psum_scatter(wide_part, "tensor", scatter_dimension=0, tiled=True)
    wide_part = wide_part.reshape(2, depth, 2, half_width)
    wide_total = by_core(half(wide_part, core_rank, 0), swap(half(wide_part, 1 - core_rank, 0)), 2).astype(F32)
    grad_first = grad_two + first_back
    grad_one, gain_one_grad, offset_one_grad = norm_backward(grad_first, normed_one, inverse_one, vectors[4])
    out_bias_grad = jnp.sum(grad_one, axis=0)
    grad_branch_one = flat(gather(unflat(grad_one.astype(BF))))
    grad_context = jnp.dot(grad_branch_one, out_turned, preferred_element_type=F32).astype(BF)
    out_grad = contract(grad_branch_one, context_flat, 0, 0)
    input_parts, qkv_grad, qkv_bias_grad = attend_backward(
        sequences, qkv_flat, qkv_rows, grad_context.reshape(context.shape), down_ids, across_ids
    )
    input_grad = unflat(grad_one + flat(scatter(input_parts.reshape(micro_count, length, model))))
    narrow_total = lax.psum_scatter(
        jnp.concatenate([qkv_grad, out_grad], axis=1).astype(BF), FSDP, scatter_dimension=0, tiled=True
    ).astype(F32)
    zero_rows = jnp.zeros((2, model), F32)
    qv_grad = lax.dynamic_update_slice_in_dim(
        zero_rows, jnp.concatenate([qkv_bias_grad[:, :head_width], qkv_bias_grad[:, 2 * head_width :]], axis=0), head_start, 1
    )
    vector_grad = jnp.concatenate(
        [
            qv_grad,
            jnp.stack(
                [
                    out_bias_grad,
                    down_bias_grad,
                    gain_one_grad,
                    offset_one_grad,
                    gain_two_grad,
                    offset_two_grad,
                ],
                axis=0,
            ),
        ],
        axis=0,
    )
    unit_grad = lax.dynamic_update_slice_in_dim(
        jnp.zeros((tensor_count, 2, half_width), F32), unit_part.reshape(tensor_count, 1, half_width), core_rank, 1
    )
    small = sum_everywhere(jnp.concatenate([vector_grad, unit_grad.reshape(-1, model)], axis=0))
    grad_totals = (
        narrow_total[:, :triple].reshape(qkv_weight.shape),
        narrow_total[:, triple:].T,
        wide_total[:, 0],
        wide_total[:, 1].T,
    )
    vector_total, unit_total = small[:8], small[8:].reshape(unit_bias.shape)
    masters = (qkv_weight, out_weight, up_weight, down_weight, vectors, unit_bias)
    firsts = (qkv_first, out_first, up_first, down_first, vectors_first, unit_bias_first)
    seconds = (qkv_second, out_second, up_second, down_second, vectors_second, unit_bias_second)
    gradients = (
        grad_totals[0],
        grad_totals[1],
        grad_totals[2],
        grad_totals[3],
        vector_total,
        unit_total,
    )
    news = [
        adam_update(
            masters[place],
            firsts[place],
            seconds[place],
            gradients[place],
            LEARNING_RATES[place],
            WEIGHT_DECAYS[place],
        )
        for place in range(6)
    ]
    return (
        layer_output,
        input_grad,
        news[0][0],
        news[0][1],
        news[0][2],
        news[1][0],
        news[1][1],
        news[1][2],
        news[2][0],
        news[2][1],
        news[2][2],
        news[3][0],
        news[3][1],
        news[3][2],
        news[4][0],
        news[4][1],
        news[4][2],
        news[5][0],
        news[5][1],
        news[5][2],
    )


def solution(mesh):
    placed = (
        P(None, FSDP + ("tensor",), None),
        P(None, FSDP + ("tensor",), None),
        P(None, FSDP),
        P(FSDP, None, "tensor"),
        P(FSDP, None, "tensor"),
        P(FSDP, None, "tensor"),
        P("tensor", FSDP),
        P("tensor", FSDP),
        P("tensor", FSDP),
        P(FSDP, "tensor"),
        P(FSDP, "tensor"),
        P(FSDP, "tensor"),
        P("tensor", FSDP),
        P("tensor", FSDP),
        P("tensor", FSDP),
        P(),
        P(),
        P(),
        P(),
        P(),
        P(),
    )
    return jax.shard_map(
        shards,
        mesh=Mesh(mesh.devices.reshape(-1, 2, mesh.shape["tensor"]), ("chip", "core", "tensor")),
        in_specs=placed,
        out_specs=(
            P(None, FSDP + ("tensor",), None),
            P(None, FSDP + ("tensor",), None),
            P(FSDP, None, "tensor"),
            P(FSDP, None, "tensor"),
            P(FSDP, None, "tensor"),
            P("tensor", FSDP),
            P("tensor", FSDP),
            P("tensor", FSDP),
            P(FSDP, "tensor"),
            P(FSDP, "tensor"),
            P(FSDP, "tensor"),
            P("tensor", FSDP),
            P("tensor", FSDP),
            P("tensor", FSDP),
            P(),
            P(),
            P(),
            P(),
            P(),
            P(),
        ),
        check_vma=False,
    )
```
